32 devices in a mesh: group: 2 (over y), wide: 8 (over z, x), narrow: 2 (over core).
Axes of the slice: x: 2, y: 2, z: 4, core: 2. Of those that a mesh axis runs over, the one named last changes fastest.
Arguments:
- tokens: bfloat16 [32, 8192], P(('group', 'wide'), 'narrow'), parts along dimension 0, may hold values from -6 to 6
- up_weight: bfloat16 [8192, 2048], P('narrow', 'wide'), may hold values from -0.0625 to 0.0625
- down_weight: bfloat16 [2048, 8192], P('wide', 'narrow'), may hold values from -0.25 to 0.25
- active_blocks: int32 [4, 4], P('group'), parts along dimension 0, may hold values from 0 to 15, as said below
Outputs:
- mixed: bfloat16 [32, 8192], P(('group', 'wide'), 'narrow'), parts along dimension 0
The draws below stay inside these ranges and needn't reach their ends.
There are 2 independent parts, one for each index of `group`. The reference program is written for one: setup_inputs(seed, part) draws one part's arguments, and reference() takes and returns one part's arrays. A program takes and returns all parts, laid end to end along the dimension named above; an argument that names none is the same for every part. Nothing has to cross between parts.
Inputs may be any that keep to these rules, and one draw needn't show every extreme that they name: `active_blocks`: each row names 4 different blocks; some blocks are active in far more tiles than others.
All inputs are finite; a program needn't handle non-finite values.
Results may differ from the reference program's by a relative error of at most 0.005.
Values may be sent and summed in bfloat16 or wider, within the bound.
A program may use at most 64 MiB of HBM per device.

```python
import jax
import jax.numpy as jnp
from jax import lax

D = 8192
BLOCK = 128
TILE = 8
FF = 2048
NBLK = 16
ACT = 4
TOKENS = 16
TILES = 2


def draw_active_blocks(key, part):
    key = jax.random.fold_in(key, 7)
    first_key, second_key = jax.random.split(key)
    popular = jax.random.randint(first_key, (NBLK,), 0, 8)
    jitter = jax.random.randint(second_key, (TILES, NBLK), 0, 16384)
    scores = (popular[None, :] * 4096 + jitter) * 1024 + jnp.arange(NBLK, dtype=jnp.int32)[None, :]
    values, chosen = lax.top_k(scores, ACT)
    return chosen.astype(jnp.int32)


def steps_of(stream_key, extent, pieces, smallest, largest):
    level, own = 1.0, jax.random.fold_in(stream_key, 6)
    for position, shards_of in pieces:
        steps = jnp.exp(jax.random.uniform(jax.random.fold_in(own, position), (shards_of,), jnp.float32, smallest / len(pieces), largest / len(pieces)))
        level = level * jnp.repeat(steps, extent[position] // shards_of).reshape([-1 if axis == position else 1 for axis in range(len(extent))])
    return level


def centred(rng, dims, scale, limit, shards=(), held_as=jnp.bfloat16):
    array = scale * jax.random.normal(rng, dims, jnp.float32)
    if shards:
        array = array * steps_of(rng, dims, shards, -0.22, 0.18)
    return jnp.clip(array, -limit, limit).astype(held_as)


def setup_inputs(seed: int = 0, part: int = 0) -> dict:
    splits = jax.random.split(jax.random.key(seed), 5)
    own_keys = jax.random.split(jax.random.fold_in(splits[4], part), 5)
    return {
        "tokens": centred(own_keys[0], (TOKENS, D), 1.0, 6.0, ((0, 8), (1, 2))),
        "up_weight": centred(splits[1], (D, FF), D ** -0.5, 0.0625, ((0, 2), (1, 8))),
        "down_weight": centred(splits[2], (FF, D), (ACT * BLOCK) ** -0.5, 0.25, ((0, 8), (1, 2))),
        "active_blocks": draw_active_blocks(jax.random.fold_in(jax.random.fold_in(splits[4], part), 71), part),
    }


def reference(tokens, up_weight, down_weight, active_blocks):
    up_sum = jnp.dot(tokens.astype(jnp.float32), up_weight.astype(jnp.float32), precision=lax.Precision.HIGHEST)
    all_blocks = jnp.arange(NBLK, dtype=jnp.int32)
    flags = jnp.any(active_blocks[:, :, None] == all_blocks[None, None, :], axis=1)
    keeper = jnp.repeat(jnp.repeat(flags, TILE, axis=0), BLOCK, axis=1)
    hidden = jnp.where(keeper, jax.nn.silu(up_sum), jnp.float32(0.0)).astype(jnp.bfloat16)
    mixed = jnp.dot(hidden.astype(jnp.float32), down_weight.astype(jnp.float32), precision=lax.Precision.HIGHEST)
    return mixed.astype(jnp.bfloat16)
```

```python
import functools

import jax
import jax.numpy as jnp
from jax import lax
from jax.experimental import pallas as pl
from jax.experimental.pallas import tpu as pltpu
from jax.sharding import PartitionSpec as P

BLOCK = 128
CHUNKS = 2
MESH = pl.DeviceIdType.MESH


def loop(count, step):
    lax.fori_loop(0, count, lambda i, c: (step(i), c)[1], 0, unroll=count <= 8)


def kernel(
    n, tok_hbm, up_hbm, down_hbm, act_hbm, out_ref,
    slots, up, down, act, xf, part, other, sbuf, rslots,
    load_sem, gsend, grecv, nsend, nrecv, rsend, rrecv,
):
    me = lax.axis_index("wide")
    core = lax.axis_index("narrow")
    mate = {"narrow": 1 - core}
    own = tok_hbm.shape[0]
    rows = n * own
    tiles = act_hbm.shape[0]
    width = down_hbm.shape[1]
    chunk = width // CHUNKS

    tok_in = pltpu.make_async_copy(tok_hbm, slots.at[me], load_sem.at[0])
    act_in = pltpu.make_async_copy(act_hbm, act, load_sem.at[1])
    up_in = pltpu.make_async_copy(up_hbm, up, load_sem.at[2])
    down_in = pltpu.make_async_copy(down_hbm, down, load_sem.at[3])
    tok_in.start()

    barrier = pltpu.get_barrier_semaphore()

    def greet(i):
        pl.semaphore_signal(
            barrier, inc=1, device_id={"wide": lax.rem(me + 1 + i, n)}, device_id_type=MESH
        )

    loop(n - 1, greet)
    pl.semaphore_signal(barrier, inc=1, device_id=mate, device_id_type=MESH)
    up_in.start()
    act_in.start()
    down_in.start()
    tok_in.wait()
    pl.semaphore_wait(barrier, n)

    def send_tokens(i):
        pltpu.make_async_remote_copy(
            src_ref=slots.at[me], dst_ref=slots.at[me], send_sem=gsend, recv_sem=grecv,
            device_id={"wide": lax.rem(me + 1 + i, n)}, device_id_type=MESH,
        ).start()

    loop(n - 1, send_tokens)

    act_in.wait()
    masks = []
    for b in range(up.shape[1] // BLOCK):
        block = me * (up.shape[1] // BLOCK) + b
        flag = jnp.max((act[...] == block).astype(jnp.float32), axis=1, keepdims=True)
        flag = jnp.broadcast_to(flag, (tiles, BLOCK))
        masks.append(
            jnp.broadcast_to(flag[:, None, :], (tiles, rows // tiles, BLOCK)).reshape(rows, BLOCK)
        )
    keeper = jnp.concatenate(masks, axis=1)

    up_in.wait()
    most = slots.at[pl.ds(0, n - 1)]
    pltpu.make_async_copy(most, most, grecv).wait()

    for j in range(n):
        xf[j * own : (j + 1) * own, :] = slots[j].astype(jnp.float32)
    part[...] = jnp.dot(
        xf[...].astype(jnp.bfloat16), up[...], preferred_element_type=jnp.float32
    )
    swap = pltpu.make_async_remote_copy(
        src_ref=part, dst_ref=other, send_sem=nsend, recv_sem=nrecv,
        device_id=mate, device_id_type=MESH,
    )
    swap.start()
    down_in.wait()
    swap.wait_recv()
    total = part[...] + other[...]
    hidden = jnp.where(keeper > 0.0, total / (1.0 + jnp.exp(-total)), 0.0).astype(jnp.bfloat16)

    for c in range(CHUNKS):
        cols = pl.ds(c * chunk, chunk)
        mix = jnp.dot(hidden, down[:, cols], preferred_element_type=jnp.float32)
        for j in range(n):
            sbuf[j, :, cols] = mix[j * own : (j + 1) * own].astype(jnp.bfloat16)

        def send_part(i):
            peer = lax.rem(me + 1 + i, n)
            pltpu.make_async_remote_copy(
                src_ref=sbuf.at[peer, :, cols], dst_ref=rslots.at[i, :, cols],
                send_sem=rsend.at[c], recv_sem=rrecv.at[c],
                device_id={"wide": peer}, device_id_type=MESH,
            ).start()

        loop(n - 1, send_part)

    for c in range(CHUNKS):
        cols = pl.ds(c * chunk, chunk)
        got = rslots.at[:, :, cols]
        pltpu.make_async_copy(got, got, rrecv.at[c]).wait()
        out_ref[:, cols] = lax.fori_loop(
            0, n - 1, lambda i, s: s + rslots[i, :, cols].astype(jnp.float32),
            sbuf[me, :, cols].astype(jnp.float32), unroll=n <= 8,
        ).astype(out_ref.dtype)

    pltpu.make_async_copy(most, most, gsend).wait()
    swap.wait_send()
    for c in range(CHUNKS):
        sent = rslots.at[:, :, pl.ds(c * chunk, chunk)]
        pltpu.make_async_copy(sent, sent, rsend.at[c]).wait()


def body(n, tokens, up_weight, down_weight, active_blocks):
    own, width = tokens.shape
    rows = n * own
    local = up_weight.shape[1]
    dma = pltpu.SemaphoreType.DMA
    return pl.pallas_call(
        functools.partial(kernel, n),
        out_shape=jax.ShapeDtypeStruct((own, width), jnp.bfloat16),
        in_specs=[pl.BlockSpec(memory_space=pltpu.HBM)] * 4,
        out_specs=pl.BlockSpec(memory_space=pltpu.VMEM),
        scratch_shapes=[
            pltpu.VMEM((n, own, width), jnp.bfloat16),
            pltpu.VMEM(up_weight.shape, jnp.bfloat16),
            pltpu.VMEM(down_weight.shape, jnp.bfloat16),
            pltpu.VMEM(active_blocks.shape, jnp.int32),
            pltpu.VMEM((rows, width), jnp.float32),
            pltpu.VMEM((rows, local), jnp.float32),
            pltpu.VMEM((rows, local), jnp.float32),
            pltpu.VMEM((n, own, width), jnp.bfloat16),
            pltpu.VMEM((n - 1, own, width), jnp.bfloat16),
            dma((4,)), dma, dma, dma, dma, dma((CHUNKS,)), dma((CHUNKS,)),
        ],
        compiler_params=pltpu.CompilerParams(
            collective_id=0, has_side_effects=True, vmem_limit_bytes=64 * 1024 * 1024 - 65536
        ),
    )(tokens, up_weight, down_weight, active_blocks)


def solution(mesh):
    in_specs = (
        P(("group", "wide"), "narrow"),
        P("narrow", "wide"),
        P("wide", "narrow"),
        P("group", None),
    )
    out_specs = P(("group", "wide"), "narrow")
    return jax.shard_map(
        functools.partial(body, mesh.shape["wide"]),
        mesh=mesh, in_specs=in_specs, out_specs=out_specs, check_vma=False,
    )
```

```python
import functools

import jax
import jax.numpy as jnp
from jax import lax
from jax.experimental import pallas as pl
from jax.experimental.pallas import tpu as pltpu
from jax.sharding import PartitionSpec as P

BLOCK = 128
CHUNKS = 1
MESH = pl.DeviceIdType.MESH


def loop(count, step):
    if count <= 8:
        for i in range(count):
            step(i)
        return
    lax.fori_loop(0, count, lambda i, c: (step(i), c)[1], 0)


def kernel(
    n, tok_hbm, up_hbm, down_hbm, act_hbm, rslots,
    slots, up, down, act, xf, part, other, sbuf,
    load_sem, gsend, grecv, nsend, nrecv, rsend, rrecv,
):
    me = lax.axis_index("wide")
    core = lax.axis_index("narrow")
    mate = {"narrow": 1 - core}
    own = tok_hbm.shape[0]
    rows = n * own
    tiles = act_hbm.shape[0]
    width = down_hbm.shape[1]
    chunk = width // CHUNKS

    def flip(d):
        bits = [lax.rem(me // 2**k, 2) for k in range(3)]
        return sum((1 - b if d // 2**k % 2 else b) * 2**k for k, b in enumerate(bits))

    def partner(i):
        return flip(n - 1 - i) if n == 8 else lax.rem(me + 1 + i, n)

    tok_in = pltpu.make_async_copy(tok_hbm, slots.at[me], load_sem.at[0])
    act_in = pltpu.make_async_copy(act_hbm, act, load_sem.at[1])
    up_in = pltpu.make_async_copy(up_hbm, up, load_sem.at[2])
    down_in = pltpu.make_async_copy(down_hbm, down, load_sem.at[3])
    tok_in.start()

    barrier = pltpu.get_barrier_semaphore()

    def greet(i):
        pl.semaphore_signal(
            barrier, inc=1, device_id={"wide": partner(i)}, device_id_type=MESH
        )

    loop(n - 1, greet)
    pl.semaphore_signal(barrier, inc=1, device_id=mate, device_id_type=MESH)
    up_in.start()
    act_in.start()
    down_in.start()
    tok_in.wait()
    pl.semaphore_wait(barrier, n)

    def send_tokens(i):
        pltpu.make_async_remote_copy(
            src_ref=slots.at[me], dst_ref=slots.at[me], send_sem=gsend, recv_sem=grecv,
            device_id={"wide": partner(i)}, device_id_type=MESH,
        ).start()

    loop(n - 1, send_tokens)

    act_in.wait()
    masks = []
    for b in range(up.shape[1] // BLOCK):
        block = me * (up.shape[1] // BLOCK) + b
        flag = jnp.max((act[...] == block).astype(jnp.float32), axis=1, keepdims=True)
        flag = jnp.broadcast_to(flag, (tiles, BLOCK))
        masks.append(
            jnp.broadcast_to(flag[:, None, :], (tiles, rows // tiles, BLOCK)).reshape(rows, BLOCK)
        )
    keeper = jnp.concatenate(masks, axis=1)

    up_in.wait()
    most = slots.at[pl.ds(0, n - 1)]
    pltpu.make_async_copy(most, most, grecv).wait()

    for j in range(n):
        xf[j * own : (j + 1) * own, :] = slots[j].astype(jnp.float32)
    part[...] = jnp.dot(
        xf[...].astype(jnp.bfloat16), up[...], preferred_element_type=jnp.float32
    )
    swap = pltpu.make_async_remote_copy(
        src_ref=part, dst_ref=other, send_sem=nsend, recv_sem=nrecv,
        device_id=mate, device_id_type=MESH,
    )
    swap.start()
    down_in.wait()
    swap.wait_recv()
    total = part[...] + other[...]
    hidden = jnp.where(keeper > 0.0, total / (1.0 + jnp.exp(-total)), 0.0).astype(jnp.bfloat16)

    for c in range(CHUNKS):
        cols = pl.ds(c * chunk, chunk)
        mix = jnp.dot(hidden, down[:, cols], preferred_element_type=jnp.float32)
        for j in range(n):
            sbuf[j, :, cols] = mix[j * own : (j + 1) * own].astype(jnp.bfloat16)

        def send_part(i):
            peer = partner(i)
            pltpu.make_async_remote_copy(
                src_ref=sbuf.at[peer, :, cols], dst_ref=rslots.at[i, :, cols],
                send_sem=rsend.at[c], recv_sem=rrecv.at[c],
                device_id={"wide": peer}, device_id_type=MESH,
            ).start()

        loop(n - 1, send_part)

    keep = pltpu.make_async_copy(sbuf.at[me], rslots.at[n - 1], load_sem.at[0])
    keep.start()
    for c in range(CHUNKS):
        cols = pl.ds(c * chunk, chunk)
        got = rslots.at[pl.ds(0, n - 1), :, cols]
        pltpu.make_async_copy(got, got, rrecv.at[c]).wait()
    pltpu.make_async_copy(most, most, gsend).wait()
    swap.wait_send()
    keep.wait()
    for c in range(CHUNKS):
        sent = rslots.at[pl.ds(0, n - 1), :, pl.ds(c * chunk, chunk)]
        pltpu.make_async_copy(sent, sent, rsend.at[c]).wait()


def body(n, tokens, up_weight, down_weight, active_blocks):
    own, width = tokens.shape
    rows = n * own
    local = up_weight.shape[1]
    dma = pltpu.SemaphoreType.DMA
    terms = pl.pallas_call(
        functools.partial(kernel, n),
        out_shape=jax.ShapeDtypeStruct((n, own, width), jnp.bfloat16),
        in_specs=[pl.BlockSpec(memory_space=pltpu.HBM)] * 4,
        out_specs=pl.BlockSpec(memory_space=pltpu.HBM),
        scratch_shapes=[
            pltpu.VMEM((n, own, width), jnp.bfloat16),
            pltpu.VMEM(up_weight.shape, jnp.bfloat16),
            pltpu.VMEM(down_weight.shape, jnp.bfloat16),
            pltpu.VMEM(active_blocks.shape, jnp.int32),
            pltpu.VMEM((rows, width), jnp.float32),
            pltpu.VMEM((rows, local), jnp.float32),
            pltpu.VMEM((rows, local), jnp.float32),
            pltpu.VMEM((n, own, width), jnp.bfloat16),
            dma((4,)), dma, dma, dma, dma, dma((CHUNKS,)), dma((CHUNKS,)),
        ],
        compiler_params=pltpu.CompilerParams(
            collective_id=0, has_side_effects=True, vmem_limit_bytes=64 * 1024 * 1024 - 65536
        ),
    )(tokens, up_weight, down_weight, active_blocks)
    return jnp.sum(terms.astype(jnp.float32), axis=0).astype(jnp.bfloat16)


def solution(mesh):
    in_specs = (
        P(("group", "wide"), "narrow"),
        P("narrow", "wide"),
        P("wide", "narrow"),
        P("group", None),
    )
    out_specs = P(("group", "wide"), "narrow")
    return jax.shard_map(
        functools.partial(body, mesh.shape["wide"]),
        mesh=mesh, in_specs=in_specs, out_specs=out_specs, check_vma=False,
    )
```

```python
import functools

import jax
import jax.numpy as jnp
from jax import lax
from jax.experimental import pallas as pl
from jax.experimental.pallas import tpu as pltpu
from jax.sharding import PartitionSpec as P

BLOCK = 128
CHUNKS = 1
MESH = pl.DeviceIdType.MESH


def loop(count, step):
    if count <= 8:
        for i in range(count):
            step(i)
        return
    lax.fori_loop(0, count, lambda i, c: (step(i), c)[1], 0)


def kernel(
    n, tok_hbm, up_hbm, down_hbm, act_hbm, rslots,
    slots, up, down, act, xf, part, other, sbuf,
    load_sem, gsend, grecv, nsend, nrecv, rsend, rrecv,
):
    me = lax.axis_index("wide")
    core = lax.axis_index("narrow")
    group = lax.axis_index("group")
    mate = (group, me, 1 - core)
    own = tok_hbm.shape[0]
    rows = n * own
    tiles = act_hbm.shape[0]
    width = down_hbm.shape[1]
    chunk = width // CHUNKS

    bits = [lax.rem(me // 2**k, 2) for k in range(3)]

    def flip(d):
        return sum((1 - b if d // 2**k % 2 else b) * 2**k for k, b in enumerate(bits))

    peers = [flip(n - 1 - i) for i in range(n - 1)] if n == 8 else None

    def partner(i):
        return peers[i] if n == 8 else lax.rem(me + 1 + i, n)

    tok_in = pltpu.make_async_copy(tok_hbm, slots.at[me], load_sem.at[0])
    act_in = pltpu.make_async_copy(act_hbm, act, load_sem.at[1])
    up_in = pltpu.make_async_copy(up_hbm, up, load_sem.at[2])
    down_in = pltpu.make_async_copy(down_hbm, down, load_sem.at[3])
    tok_in.start()

    barrier = pltpu.get_barrier_semaphore()

    def greet(i):
        pl.semaphore_signal(
            barrier, inc=1, device_id=(group, partner(i), core), device_id_type=MESH
        )

    loop(n - 1, greet)
    pl.semaphore_signal(barrier, inc=1, device_id=mate, device_id_type=MESH)
    up_in.start()
    act_in.start()
    down_in.start()
    tok_in.wait()
    pl.semaphore_wait(barrier, n)

    def send_tokens(i):
        pltpu.make_async_remote_copy(
            src_ref=slots.at[me], dst_ref=slots.at[me], send_sem=gsend, recv_sem=grecv,
            device_id=(group, partner(i), core), device_id_type=MESH,
        ).start()

    loop(n - 1, send_tokens)

    act_in.wait()
    masks = []
    for b in range(up.shape[1] // BLOCK):
        block = me * (up.shape[1] // BLOCK) + b
        flag = jnp.max((act[...] == block).astype(jnp.float32), axis=1, keepdims=True)
        flag = jnp.broadcast_to(flag, (tiles, BLOCK))
        if n == 8:
            tall = rows // tiles
            place = lax.broadcasted_iota(jnp.int32, (rows, BLOCK), 0) // own
            owner = jnp.where(place == n - 1, me, 0)
            for i, peer in enumerate(peers):
                owner = jnp.where(place == i, peer, owner)
            row = owner * own + lax.broadcasted_iota(jnp.int32, (rows, BLOCK), 0) % own
            mask = jnp.zeros((rows, BLOCK), jnp.float32)
            for t in range(tiles):
                mask = jnp.where(row // tall == t, flag[t : t + 1], mask)
            masks.append(mask)
        else:
            masks.append(
                jnp.broadcast_to(flag[:, None, :], (tiles, rows // tiles, BLOCK)).reshape(rows, BLOCK)
            )
    keeper = jnp.concatenate(masks, axis=1)

    up_in.wait()
    most = slots.at[pl.ds(0, n - 1)]
    pltpu.make_async_copy(most, most, grecv).wait()

    ranks = [*peers, me] if n == 8 else list(range(n))
    for j, owner in enumerate(ranks):
        xf[j * own : (j + 1) * own, :] = slots[owner].astype(jnp.float32)
    half = up.shape[1] // 2
    swaps = []
    for k in range(2):
        part[k] = jnp.dot(
            xf[...].astype(jnp.bfloat16), up[:, k * half : (k + 1) * half],
            preferred_element_type=jnp.float32,
        )
        swap = pltpu.make_async_remote_copy(
            src_ref=part.at[k], dst_ref=other.at[k], send_sem=nsend.at[k], recv_sem=nrecv.at[k],
            device_id=mate, device_id_type=MESH,
        )
        swap.start()
        swaps.append(swap)
    down_in.wait()
    parts = []
    for k in range(2):
        swaps[k].wait_recv()
        total = part[k] + other[k]
        active = keeper[:, k * half : (k + 1) * half] > 0.0
        parts.append(jnp.where(active, total / (1.0 + jnp.exp(-total)), 0.0).astype(jnp.bfloat16))
    hidden = jnp.concatenate(parts, axis=1)

    for c in range(CHUNKS):
        cols = pl.ds(c * chunk, chunk)
        mix = jnp.dot(hidden, down[:, cols], preferred_element_type=jnp.float32)
        for j in range(n - 1 if n == 8 else 0, n):
            sbuf[j, :, cols] = mix[j * own : (j + 1) * own].astype(jnp.bfloat16)

        def send_part(i):
            peer = partner(i)
            if n == 8:
                sbuf[i, :, cols] = mix[i * own : (i + 1) * own].astype(jnp.bfloat16)
            pltpu.make_async_remote_copy(
                src_ref=sbuf.at[i if n == 8 else peer, :, cols], dst_ref=rslots.at[i, :, cols],
                send_sem=rsend.at[c], recv_sem=rrecv.at[c],
                device_id=(group, peer, core), device_id_type=MESH,
            ).start()

        loop(n - 1, send_part)

    pltpu.make_async_copy(most, most, gsend).wait()
    for swap in swaps:
        swap.wait_send()
    keep = pltpu.make_async_copy(sbuf.at[n - 1 if n == 8 else me], rslots.at[n - 1], load_sem.at[0])
    keep.start()
    for c in range(CHUNKS):
        cols = pl.ds(c * chunk, chunk)
        got = rslots.at[pl.ds(0, n - 1), :, cols]
        pltpu.make_async_copy(got, got, rrecv.at[c]).wait()
    keep.wait()
    for c in range(CHUNKS):
        sent = rslots.at[pl.ds(0, n - 1), :, pl.ds(c * chunk, chunk)]
        pltpu.make_async_copy(sent, sent, rsend.at[c]).wait()


def body(n, tokens, up_weight, down_weight, active_blocks):
    own, width = tokens.shape
    rows = n * own
    local = up_weight.shape[1]
    dma = pltpu.SemaphoreType.DMA
    terms = pl.pallas_call(
        functools.partial(kernel, n),
        out_shape=jax.ShapeDtypeStruct((n, own, width), jnp.bfloat16),
        in_specs=[pl.BlockSpec(memory_space=pltpu.HBM)] * 4,
        out_specs=pl.BlockSpec(memory_space=pltpu.HBM),
        scratch_shapes=[
            pltpu.VMEM((n, own, width), jnp.bfloat16),
            pltpu.VMEM(up_weight.shape, jnp.bfloat16),
            pltpu.VMEM(down_weight.shape, jnp.bfloat16),
            pltpu.VMEM(active_blocks.shape, jnp.int32),
            pltpu.VMEM((rows, width), jnp.float32),
            pltpu.VMEM((2, rows, local // 2), jnp.float32),
            pltpu.VMEM((2, rows, local // 2), jnp.float32),
            pltpu.VMEM((n, own, width), jnp.bfloat16),
            dma((4,)), dma, dma, dma((2,)), dma((2,)), dma((CHUNKS,)), dma((CHUNKS,)),
        ],
        compiler_params=pltpu.CompilerParams(
            collective_id=0, has_side_effects=True, vmem_limit_bytes=64 * 1024 * 1024 - 65536
        ),
    )(tokens, up_weight, down_weight, active_blocks)
    return jnp.sum(terms.astype(jnp.float32), axis=0).astype(jnp.bfloat16)


def solution(mesh):
    in_specs = (
        P(("group", "wide"), "narrow"),
        P("narrow", "wide"),
        P("wide", "narrow"),
        P("group", None),
    )
    out_specs = P(("group", "wide"), "narrow")
    return jax.shard_map(
        functools.partial(body, mesh.shape["wide"]),
        mesh=mesh, in_specs=in_specs, out_specs=out_specs, check_vma=False,
    )
```
